32 devices in a mesh: row: 4 (over z), col: 8 (over y, x, core).
Axes of the slice: x: 2, y: 2, z: 4, core: 2. Of those that a mesh axis runs over, the one named last changes fastest.
Arguments:
- covariance: float32 [16384, 16384], P('row', 'col'), as said below
- fields: float32 [512, 16384], P('col', 'row'), may hold values from -6 to 6
Outputs:
- factored: float32 [16384, 16384], P('row', 'col')
- solved_fields: float32 [512, 16384], P('col', 'row')
The draws below stay inside these ranges and needn't reach their ends.
Inputs may be any that keep to these rules, and one draw needn't show every extreme that they name: covariance, read in the global order of the steps, is symmetric positive definite.
All inputs are finite; a program needn't handle non-finite values.
Results may differ from the reference program's by a relative error of at most 0.0003.
Values sent between devices are 32-bit elements; how exact they have to be, the bound alone decides.
A program may use at most 192 MiB of HBM per device.

```python
import math
import jax
import jax.numpy as jnp
from jax import lax

ORDER = 16384
NB = 512
FIELDS = 512
ROWS_DEV = 4096
COLS_DEV = 2048
BLOCK = 64
N_ROW = 4
N_COL = 8


NUGGET = 0.3


RANGE = 0.1


def stored_to_global(count, block, groups):
    stored = jnp.arange(count, dtype=jnp.int32)
    share = count // groups
    return (stored % share // block * groups + stored // share) * block + stored % block


def draw_covariance(key, part):
    block = NB // N_COL
    points = jax.random.uniform(jax.random.fold_in(key, 11), (ORDER, 2), jnp.float32)
    rows_global = stored_to_global(ORDER, block, N_ROW)
    cols_global = stored_to_global(ORDER, block, N_COL)
    col_points = points[cols_global]
    stretch = math.sqrt(3.0) / RANGE
    height = math.gcd(ORDER, 1024)

    def one_block(row_ids):
        row_points = points[row_ids]
        delta_x = row_points[:, 0:1] - col_points[None, :, 0]
        delta_y = row_points[:, 1:2] - col_points[None, :, 1]
        scaled = jnp.sqrt(delta_x * delta_x + delta_y * delta_y) * stretch
        kernel = (1.0 + scaled) * jnp.exp(-scaled)
        kernel = kernel + jnp.where(row_ids[:, None] == cols_global[None, :], NUGGET, 0.0)
        return kernel
    blocks = lax.map(one_block, rows_global.reshape(ORDER // height, height))
    return blocks.reshape(ORDER, ORDER).astype(jnp.float32)


def levels(own_key, shape, cuts, smallest, high):
    def one(position, parts):
        heights = jax.random.uniform(jax.random.fold_in(jax.random.fold_in(own_key, 6), position), (parts,), jnp.float32, smallest / len(cuts), high / len(cuts))
        return jnp.repeat(jnp.exp(heights), shape[position] // parts).reshape((-1,) + (1,) * (len(shape) - position - 1))

    factor_of = one(*cuts[0])
    for cut in cuts[1:]:
        factor_of = factor_of * one(*cut)
    return factor_of


def normal_values(key, extent, scale, most, shards=(), held_as=jnp.bfloat16):
    values = scale * jax.random.normal(key, extent, jnp.float32)
    if shards:
        values = values * levels(key, extent, shards, -0.22, 0.18)
    return jnp.clip(values, -most, most).astype(held_as)


def setup_inputs(seed: int = 0) -> dict:
    streams_of = jax.random.split(jax.random.key(seed), 3)
    return {
        "covariance": draw_covariance(jax.random.fold_in(streams_of[2], 71), 0),
        "fields": normal_values(streams_of[1], (FIELDS, ORDER), 1.0, 6.0, ((0, 8), (1, 4)), jnp.float32),
    }


PRECISE = lax.Precision.HIGHEST

def reference(covariance, fields):
    matrix = covariance.reshape(N_ROW, ROWS_DEV // BLOCK, BLOCK, N_COL, COLS_DEV // BLOCK, BLOCK)
    matrix = matrix.transpose(1, 0, 2, 4, 3, 5).reshape(ORDER, ORDER)
    field_rows = fields.reshape(FIELDS, N_ROW, ROWS_DEV // BLOCK, BLOCK).transpose(0, 2, 1, 3).reshape(FIELDS, ORDER)
    positions = jnp.arange(ORDER, dtype=jnp.int32)[:, None]
    panels = []
    for step in range(2):
        lower = step * NB
        higher = lower + NB
        factor = jnp.linalg.cholesky(matrix[lower:higher, lower:higher])
        inverse = jax.scipy.linalg.solve_triangular(factor, jnp.eye(NB, dtype=matrix.dtype), lower=True)
        product = jnp.dot(matrix[:, lower:higher], inverse.T, precision=PRECISE)
        column = jnp.where(positions < lower, 0.0, product).at[lower:higher].set(factor)
        trail = jnp.where(positions >= higher, column, 0.0)
        solved = jnp.dot(field_rows[:, lower:higher], inverse.T, precision=PRECISE)
        field_rows = (field_rows - jnp.dot(solved, trail.T, precision=PRECISE)).at[:, lower:higher].set(solved)
        matrix = matrix.at[:, higher:].add(-jnp.dot(trail, trail[higher:].T, precision=PRECISE))
        panels.append(column)
    remainder = jnp.where(positions < 2 * NB, 0.0, matrix[:, 2 * NB:])
    matrix = jnp.concatenate([panels[0], panels[1], remainder], axis=1)
    matrix = matrix.reshape(ROWS_DEV // BLOCK, N_ROW, BLOCK, COLS_DEV // BLOCK, N_COL, BLOCK)
    factored = matrix.transpose(1, 0, 2, 4, 3, 5).reshape(ORDER, ORDER)
    solved_fields = field_rows.reshape(FIELDS, ROWS_DEV // BLOCK, N_ROW, BLOCK).transpose(0, 2, 1, 3).reshape(FIELDS, ORDER)
    return (factored, solved_fields)
```

```python
import functools

import jax
import jax.numpy as jnp
from jax import lax
from jax.experimental import pallas as pl
from jax.experimental.pallas import tpu as pltpu
from jax.sharding import PartitionSpec as P

NB = 512

EXACT = lax.Precision.HIGHEST
PANEL = lax.Precision.HIGH


def dot(left, right, left_axis, right_axis, precision):
    return lax.dot_general(
        left,
        right,
        (((left_axis,), (right_axis,)), ((), ())),
        precision=precision,
        preferred_element_type=jnp.float32,
    )


def split(value):
    high = value.astype(jnp.bfloat16)
    return high, (value - high.astype(jnp.float32)).astype(jnp.bfloat16)


def update_kernel(top, width, chunk, a_ref, p0_ref, p1_ref, q0_ref, q1_ref, edge_ref, o_ref, high, low):
    tile, columns = a_ref.shape
    step = pl.program_id(0)

    @pl.when(step == 0)
    def _():
        for k, ref in enumerate((q0_ref, q1_ref)):
            for at in range(0, NB, 64):
                upper, lower = split(ref[at : at + 64, :])
                high[k * NB + at : k * NB + at + 64, :] = upper
                low[k * NB + at : k * NB + at + 64, :] = lower

    p_high, p_low = split(jnp.concatenate([p0_ref[...], p1_ref[...]], axis=1))
    rows = step * tile + lax.broadcasted_iota(jnp.int32, (tile, chunk), 0)
    for at in range(0, columns, chunk):
        here = slice(at, at + chunk)
        right_high = high[:, here]
        total = jnp.dot(p_high, right_high, preferred_element_type=jnp.float32)
        total += jnp.dot(p_low, right_high, preferred_element_type=jnp.float32)
        total += jnp.dot(p_high, low[:, here], preferred_element_type=jnp.float32)
        o_ref[:, here] = jnp.where(rows < top, 0.0, a_ref[:, here] - total)
    o_ref[:, :width] = edge_ref[...]


def update(matrix, p0, p1, q0, q1, edge, top):
    rows, columns = matrix.shape
    tile = min(256, rows)
    chunk = min(512, columns)
    width = edge.shape[1]
    return pl.pallas_call(
        functools.partial(update_kernel, top, width, chunk),
        grid=(rows // tile,),
        out_shape=jax.ShapeDtypeStruct(matrix.shape, jnp.float32),
        in_specs=[
            pl.BlockSpec((tile, columns), lambda i: (i, 0)),
            pl.BlockSpec((tile, NB), lambda i: (i, 0)),
            pl.BlockSpec((tile, NB), lambda i: (i, 0)),
            pl.BlockSpec((NB, columns), lambda i: (0, 0)),
            pl.BlockSpec((NB, columns), lambda i: (0, 0)),
            pl.BlockSpec((tile, width), lambda i: (i, 0)),
        ],
        out_specs=pl.BlockSpec((tile, columns), lambda i: (i, 0)),
        scratch_shapes=[
            pltpu.VMEM((2 * NB, columns), jnp.bfloat16),
            pltpu.VMEM((2 * NB, columns), jnp.bfloat16),
        ],
        compiler_params=pltpu.CompilerParams(vmem_limit_bytes=56 * 1024 * 1024),
        cost_estimate=pl.CostEstimate(
            flops=12 * NB * rows * columns, bytes_accessed=8 * rows * columns, transcendentals=0
        ),
    )(matrix, p0, p1, q0, q1, edge)


def factor_block(square):
    factor = jnp.linalg.cholesky(square)
    inverse = jax.scipy.linalg.solve_triangular(factor, jnp.eye(NB, dtype=jnp.float32), lower=True)
    return factor, inverse


def shards(covariance, fields):
    row_count = lax.axis_size("row")
    column_count = lax.axis_size("col")
    row_index = lax.axis_index("row")
    column_index = lax.axis_index("col")
    local_rows, local_columns = covariance.shape
    width_fields = fields.shape[0]
    block = NB // column_count
    ratio = column_count // row_count
    stripe = ratio * block

    def order_rows(stacked, steps):
        tail = stacked.shape[1]
        stacked = stacked.reshape(row_count, steps * ratio, block, tail)
        return stacked.transpose(1, 0, 2, 3).reshape(steps * NB, tail)

    def own_rows(value):
        return own_rows_of(value, ratio, row_count, block, row_index)

    def corner(piece, steps):
        across = lax.all_gather(piece, "col", axis=1, tiled=True)
        return order_rows(lax.all_gather(across, "row", axis=0, tiled=True), steps)

    first = corner(covariance[:stripe, :block], 1)
    second = corner(covariance[: 2 * stripe, block : 2 * block], 2)
    panel = lax.all_gather(covariance[:, : 2 * block].T, "col", axis=0, tiled=True)
    panel = panel.reshape(column_count, 2, block, local_rows).transpose(1, 0, 2, 3)
    panel = panel.reshape(2, NB, local_rows)
    across = order_rows(lax.all_gather(covariance[: 2 * stripe], "row", axis=0, tiled=True), 2)
    strip = order_rows(lax.all_gather(fields[:, : 2 * stripe].T, "row", axis=0, tiled=True), 2)

    factor0, inverse0 = factor_block(first)
    side = dot(inverse0, second[:NB], 1, 0, EXACT)
    factor1, inverse1 = factor_block(second[NB:] - dot(side, side, 0, 0, EXACT))

    p0 = dot(panel[0], inverse0, 0, 1, PANEL)
    p1 = dot(panel[1].T - dot(p0, side, 1, 0, PANEL), inverse1, 1, 1, PANEL)
    q0 = dot(inverse0, across[:NB], 1, 0, PANEL)
    q1 = dot(inverse1, across[NB:] - dot(side, q0, 0, 0, PANEL), 1, 0, PANEL)
    y0 = dot(inverse0, strip[:NB], 1, 0, EXACT)
    y1 = dot(inverse1, strip[NB:] - dot(side, y0, 0, 0, EXACT), 1, 0, EXACT)

    start = column_index * block
    edge0 = lax.dynamic_slice_in_dim(p0, start, block, 1)
    edge1 = lax.dynamic_slice_in_dim(p1, start, block, 1)
    own0 = lax.dynamic_slice_in_dim(own_rows(factor0), start, block, 1)
    own1 = lax.dynamic_slice_in_dim(own_rows(factor1), start, block, 1)
    edge0 = jnp.concatenate([own0, edge0[stripe:]], axis=0)
    edge1 = jnp.concatenate([jnp.zeros_like(own1), own1, edge1[2 * stripe :]], axis=0)
    edge = jnp.concatenate([edge0, edge1], axis=1)
    factored = update(covariance, p0, p1, q0, q1, edge, 2 * stripe)

    moved = fields - dot(y0, p0, 0, 1, PANEL) - dot(y1, p1, 0, 1, PANEL)
    head = [own_rows(y0), own_rows(y1)]
    solved = jnp.concatenate([head[0].T, head[1].T, moved[:, 2 * stripe :]], axis=1)
    return (factored, solved)


def own_rows_of(value, ratio, row_count, block, row_index):
    tail = value.shape[1]
    picked = lax.dynamic_index_in_dim(
        value.reshape(ratio, row_count, block, tail), row_index, 1, keepdims=False
    )
    return picked.reshape(ratio * block, tail)


def solution(mesh):
    return jax.shard_map(
        shards,
        mesh=mesh,
        in_specs=(P("row", "col"), P("col", "row")),
        out_specs=(P("row", "col"), P("col", "row")),
        check_vma=False,
    )
```
